768 devices in a mesh: row: 64 (over y, x, core), col: 12 (over z).
Axes of the slice: x: 4, y: 8, z: 12, core: 2. Of those that a mesh axis runs over, the one named last changes fastest.
Arguments:
- matrix: float32 [9216, 9216], P('row', 'col'), as said below
Outputs:
- factored: float32 [9216, 9216], P('row', 'col')
Inputs may be any that keep to these rules, and one draw needn't show every extreme that they name: `matrix`: Off-diagonal entries are of order one; each diagonal entry lies between 4 * sqrt(256) and 8 * sqrt(256) times that.
All inputs are finite; a program needn't handle non-finite values.
Results may differ from the reference program's by a relative error of at most 0.0001.
Values sent between devices are 32-bit elements; how exact they have to be, the bound alone decides.
A program may use at most 32 MiB of HBM per device.

```python
import jax
import jax.numpy as jnp
from jax import lax

N = 9216
B = 256
STEPS = 2


def draw_matrix(key, part):
    key_off, key_diag = jax.random.split(key)
    offdiag = jax.random.normal(key_off, (N, N), jnp.float32)
    scale = 4.0 * jnp.sqrt(jnp.float32(B))
    diagonal = scale * jax.random.uniform(key_diag, (N,), jnp.float32, 1.0, 2.0)
    indices = jnp.arange(N, dtype=jnp.int32)
    return jnp.where(indices[:, None] == indices[None, :], diagonal[:, None], offdiag)


def setup_inputs(seed: int = 0) -> dict:
    streams_of = jax.random.split(jax.random.key(seed), 2)
    matrix = draw_matrix(jax.random.fold_in(streams_of[1], 71), 0)
    return {"matrix": matrix}


def mult(left, right):
    return jnp.dot(left, right, precision=lax.Precision.HIGHEST, preferred_element_type=jnp.float32)


def reference(matrix):
    work = matrix
    row_ids = jnp.arange(N, dtype=jnp.int32)[:, None]
    col_ids = jnp.arange(N, dtype=jnp.int32)[None, :]
    eye = jnp.eye(B, dtype=jnp.float32)
    for step in range(STEPS):
        lead = step * B
        block = work[lead:lead + B, lead:lead + B]
        panel = work[:, lead:lead + B]
        upper = work[lead:lead + B, :]
        inverse = 1.0 / jnp.diagonal(block)
        first = inverse[:, None] * (2.0 * eye - block * inverse[None, :])
        second = mult(first, 2.0 * eye - mult(block, first))
        lower = mult(panel, second)
        update = mult(lower, upper)
        picked = jnp.take(lower, jnp.clip(col_ids[0] - lead, 0, B - 1), axis=1)
        below = row_ids >= lead + B
        right = col_ids >= lead + B
        inside = (col_ids >= lead) & (col_ids < lead + B)
        work = jnp.where(below & right, work - update, jnp.where(below & inside, picked, work))
    return work
```

```python
import jax
import jax.numpy as jnp
from jax import lax
from jax.experimental import pallas as pl
from jax.experimental.pallas import tpu as pltpu
from jax.sharding import PartitionSpec as P

B = 256
ROWS, COLS = 144, 768
NX, NY, NZ = 4, 8, 12
CH = 16
NCH = ROWS // CH
LAST = (2 * B - 3 * ROWS) // CH
LAG = 4
PARTS = ((0, 2 * B), (2 * B, COLS - 2 * B))
MESH = pl.DeviceIdType.MESH
F1, F2, FAR, EX, SIBP, SIBS = range(6)
RP, RX, RSP, RSS = range(4)

Y_TREE = {0: (2, 6), 2: (3, 1), 6: (5, 7), 3: (4, None)}
Z_TREE = {0: (3, 9), 3: (5, 2), 5: (6, 4), 2: (1, None), 9: (8, 10), 8: (7, None), 10: (11, None)}


def lookup(value, table):
    found = jnp.int32(0)
    entry = jnp.int32(0)
    for key, item in table.items():
        found = jnp.where(value == key, 1, found)
        entry = jnp.where(value == key, item, entry)
    return found, entry


def branch(tree, which):
    return {k: v[which] for k, v in tree.items() if v[which] is not None}


def parents(tree):
    return {child: k for k, v in tree.items() for child in v if child is not None}


def split(v):
    high = v.astype(jnp.bfloat16)
    low = (v - high.astype(jnp.float32)).astype(jnp.bfloat16)
    return high, low


def dot(a, b):
    return jnp.dot(a, b, preferred_element_type=jnp.float32)


def mult(a, b):
    ah, al = split(a)
    bh, bl = split(b)
    return dot(ah, bh) + (dot(ah, bl) + dot(al, bh))


def inverse_of(block):
    i = lax.broadcasted_iota(jnp.int32, (B, B), 0)
    j = lax.broadcasted_iota(jnp.int32, (B, B), 1)
    diag = jnp.where(i == j, block, 0.0)
    two = jnp.where(i == j, 2.0, 0.0)
    across = 1.0 / jnp.sum(diag, axis=0, keepdims=True)
    down = 1.0 / jnp.sum(diag, axis=1, keepdims=True)
    first = down * (two - block * across)
    return mult(first, two - mult(block, first))


def kernel(m_ref, o_ref, tile, ubuf, wbuf, low0, ssem, rsem, zssem, zrsem, lsem, osem):
    r = lax.axis_index("row")
    z = lax.axis_index("col")
    y, x, c = r // (2 * NX), (r // 2) % NX, r % 2
    odd = x % 2
    other = x + 1 - 2 * odd

    def at(yy, xx, cc, zz):
        return ((yy * NX + xx) * 2 + cc, zz)

    has_f1, y1 = lookup(y, branch(Y_TREE, 0))
    has_f2, y2 = lookup(y, branch(Y_TREE, 1))
    has_up, yup = lookup(y, parents(Y_TREE))
    source = jnp.where((y == 0) & (x < 2), 1, 0)
    far_in = jnp.where((y == 0) & (x >= 2), 1, 0)
    has_z1, z1 = lookup(z, branch(Z_TREE, 0))
    has_z2, z2 = lookup(z, branch(Z_TREE, 1))
    has_zup, zup = lookup(z, parents(Z_TREE))
    xfar = (x + 2) % NX

    mine = c + 2 * odd
    theirs = c + 2 - 2 * odd
    n_mine = jnp.where(mine == 3, LAST, NCH)
    n_theirs = jnp.where(theirs == 3, LAST, NCH)
    sib_p = 1 - c + 2 * odd
    sib_s = 1 - c + 2 - 2 * odd
    n_sib_p = jnp.where(sib_p == 3, LAST, NCH)
    n_sib_s = jnp.where(sib_s == 3, LAST, NCH)

    load = pltpu.make_async_copy(m_ref, tile, lsem.at[0])
    load.start()
    full = (source == 1) & (mine != 3)
    part = (source == 1) & (mine == 3)

    def own(n):
        return pltpu.make_async_copy(
            m_ref.at[pl.ds(0, n)], ubuf.at[pl.ds(pl.multiple_of(mine * ROWS, CH), n)], lsem.at[1]
        )

    @pl.when(full)
    def _():
        own(ROWS).start()

    @pl.when(part)
    def _():
        own(LAST * CH).start()

    bar = pltpu.get_barrier_semaphore()

    def hello(where):
        pl.semaphore_signal(bar, inc=1, device_id=where, device_id_type=MESH)

    @pl.when(has_up == 1)
    def _():
        hello(at(yup, x, c, z))

    @pl.when(far_in == 1)
    def _():
        hello(at(0, xfar, c, z))

    @pl.when(has_zup == 1)
    def _():
        hello((r, zup))

    hello(at(y, other, c, z))
    hello(at(y, x, 1 - c, z))
    pl.semaphore_wait(bar, 2 + has_f1 + has_f2 + source + has_z1 + has_z2)

    @pl.when(full)
    def _():
        own(ROWS).wait()

    @pl.when(part)
    def _():
        own(LAST * CH).wait()

    def rows_of(block, i):
        return pl.ds(pl.multiple_of(block * ROWS + i * CH, CH), CH)

    def copy(p, block, i, kind, got, where):
        start, width = PARTS[p]
        ref = ubuf.at[rows_of(block, i), pl.ds(start, width)]
        return pltpu.make_async_remote_copy(
            src_ref=ref,
            dst_ref=ref,
            send_sem=ssem.at[p, kind, i],
            recv_sem=rsem.at[p, got, i],
            device_id=where,
            device_id_type=MESH,
        )

    sends = (
        (F1, has_f1, RP, at(y1, x, c, z)),
        (F2, has_f2, RP, at(y2, x, c, z)),
        (FAR, source, RP, at(0, xfar, c, z)),
        (EX, None, RX, at(y, other, c, z)),
        (SIBP, None, RSP, at(y, x, 1 - c, z)),
    )
    sibling = at(y, x, 1 - c, z)

    def plane(p):
        def body(i, carry):
            @pl.when(i < n_mine)
            def _():
                @pl.when(source == 0)
                def _():
                    copy(p, mine, i, F1, RP, sibling).wait_recv()

                for kind, has, got, where in sends:
                    if has is None:
                        copy(p, mine, i, kind, got, where).start()
                    else:

                        @pl.when(has == 1)
                        def _(kind=kind, got=got, where=where):
                            copy(p, mine, i, kind, got, where).start()

            j = i - LAG

            @pl.when((j >= 0) & (j < n_theirs))
            def _():
                copy(p, theirs, j, EX, RX, sibling).wait_recv()
                copy(p, theirs, j, SIBS, RSS, sibling).start()

            return carry

        lax.fori_loop(0, NCH + LAG, body, 0)

        def got(i, carry):
            @pl.when(i < n_sib_p)
            def _():
                copy(p, sib_p, i, SIBP, RSP, sibling).wait_recv()

            @pl.when(i < n_sib_s)
            def _():
                copy(p, sib_s, i, SIBS, RSS, sibling).wait_recv()

            return carry

        lax.fori_loop(0, NCH, got, 0)

    def sent(p):
        def body(i, carry):
            @pl.when(i < n_mine)
            def _():
                for kind, has, got, where in sends:
                    if has is None:
                        copy(p, mine, i, kind, got, where).wait_send()
                    else:

                        @pl.when(has == 1)
                        def _(kind=kind, got=got, where=where):
                            copy(p, mine, i, kind, got, where).wait_send()

            @pl.when(i < n_theirs)
            def _():
                copy(p, theirs, i, SIBS, RSS, sibling).wait_send()

            return carry

        lax.fori_loop(0, NCH, body, 0)

    def wcopy(i, kind, where):
        ref = wbuf.at[pl.ds(pl.multiple_of(i * CH, CH), CH)]
        return pltpu.make_async_remote_copy(
            src_ref=ref,
            dst_ref=ref,
            send_sem=zssem.at[kind, i],
            recv_sem=zrsem.at[i],
            device_id=where,
            device_id_type=MESH,
        )

    down = ((0, has_z1, (r, z1)), (1, has_z2, (r, z2)))

    def along(i, carry):
        @pl.when(has_zup == 1)
        def _():
            wcopy(i, 0, (r, z1)).wait_recv()

        for kind, has, where in down:

            @pl.when(has == 1)
            def _(kind=kind, where=where):
                wcopy(i, kind, where).start()

        return carry

    def along_sent(i, carry):
        for kind, has, where in down:

            @pl.when(has == 1)
            def _(kind=kind, where=where):
                wcopy(i, kind, where).wait_send()

        return carry

    row_id = r * ROWS + lax.broadcasted_iota(jnp.int32, (ROWS, B), 0)
    below0 = row_id >= B
    below1 = row_id >= 2 * B

    plane(0)
    load.wait()

    @pl.when(z == 0)
    def _():
        second0 = inverse_of(ubuf[:B, :B])
        s0 = split(second0)

        def times(a, pair):
            ah, al = split(a)
            return dot(ah, pair[0]) + (dot(ah, pair[1]) + dot(al, pair[0]))

        l10 = times(ubuf[B : 2 * B, :B], s0)
        lower0 = times(tile[:, :B], s0)
        u01 = split(ubuf[:B, B : 2 * B])
        block1 = ubuf[B : 2 * B, B : 2 * B] - times(l10, u01)
        panel1 = tile[:, B : 2 * B] - times(lower0, u01)
        lower1 = mult(panel1, inverse_of(block1))
        w0 = lower0 - mult(lower1, l10)
        wbuf[:, :B] = jnp.where(below1, w0, jnp.where(below0, lower0, 0.0))
        wbuf[:, B:] = jnp.where(below1, lower1, 0.0)
        low0[...] = lower0
        tile[:, B : 2 * B] = jnp.where(below1, lower1, jnp.where(below0, panel1, tile[:, B : 2 * B]))
        lax.fori_loop(0, NCH, along, 0)

    plane(1)

    @pl.when(z != 0)
    def _():
        lax.fori_loop(0, NCH, along, 0)

    wh, wl = split(wbuf[...])

    def update(start):
        uh, ul = split(ubuf[:, start : start + B])
        tile[:, start : start + B] -= dot(wh, uh) + (dot(wh, ul) + dot(wl, uh))

    @pl.when(z != 0)
    def _():
        update(0)
        update(B)

    update(2 * B)

    @pl.when(z == 0)
    def _():
        tile[:, :B] = jnp.where(below0, low0[...], tile[:, :B])

    out = pltpu.make_async_copy(tile, o_ref, osem)
    out.start()
    sent(0)
    sent(1)
    lax.fori_loop(0, NCH, along_sent, 0)
    out.wait()


def on_device(matrix):
    return pl.pallas_call(
        kernel,
        out_shape=jax.ShapeDtypeStruct((ROWS, COLS), jnp.float32),
        in_specs=[pl.BlockSpec(memory_space=pl.ANY)],
        out_specs=pl.BlockSpec(memory_space=pl.ANY),
        scratch_shapes=[
            pltpu.VMEM((ROWS, COLS), jnp.float32),
            pltpu.VMEM((2 * B, COLS), jnp.float32),
            pltpu.VMEM((ROWS, 2 * B), jnp.float32),
            pltpu.VMEM((ROWS, B), jnp.float32),
            pltpu.SemaphoreType.DMA((2, 6, NCH)),
            pltpu.SemaphoreType.DMA((2, 4, NCH)),
            pltpu.SemaphoreType.DMA((2, NCH)),
            pltpu.SemaphoreType.DMA((NCH,)),
            pltpu.SemaphoreType.DMA((2,)),
            pltpu.SemaphoreType.DMA,
        ],
        compiler_params=pltpu.CompilerParams(
            collective_id=0, has_side_effects=True, vmem_limit_bytes=40 << 20
        ),
        name="panel_steps",
    )(matrix)


def solution(mesh):
    return jax.shard_map(
        on_device,
        mesh=mesh,
        in_specs=(P("row", "col"),),
        out_specs=P("row", "col"),
        check_vma=False,
    )
```

```python
import jax
import jax.numpy as jnp
from jax import lax
from jax.experimental import pallas as pl
from jax.experimental.pallas import tpu as pltpu
from jax.sharding import PartitionSpec as P

B = 256
ROWS, COLS = 144, 768
NX, NY, NZ = 4, 8, 12
CH = 16
NCH = ROWS // CH
CZ = 8
NCZ = ROWS // CZ
LAST = (2 * B - 3 * ROWS) // CH
PARTS = ((0, 2 * B), (2 * B, COLS - 2 * B))
MESH = pl.DeviceIdType.MESH
VMEM = 54500 << 10
F1, F2, FAR, EX, SIBP, SIBS, FAR2, G1, G2 = range(9)
RP, RX, RSP, RSS = range(4)

Y_TREE = {0: (2, 6), 2: (3, 1), 6: (5, 7), 3: (4, None)}
Z_TREE = {
    0: (1, 9),
    1: (2, None),
    2: (3, None),
    3: (4, None),
    9: (6, 10),
    10: (11, None),
    6: (5, 7),
    7: (8, None),
}
EARLY = (5, 6)
PASS_FIRST = 9


def lookup(value, table):
    found = jnp.int32(0)
    entry = jnp.int32(0)
    for key, item in table.items():
        found = jnp.where(value == key, 1, found)
        entry = jnp.where(value == key, item, entry)
    return found, entry


def branch(tree, which):
    return {k: v[which] for k, v in tree.items() if v[which] is not None}


def parents(tree):
    return {child: k for k, v in tree.items() for child in v if child is not None}


def split(v):
    high = v.astype(jnp.bfloat16)
    low = (v - high.astype(jnp.float32)).astype(jnp.bfloat16)
    return high, low


def dot(a, b):
    return jnp.dot(a, b, preferred_element_type=jnp.float32)


def mult(a, b):
    ah, al = split(a)
    bh, bl = split(b)
    return dot(ah, bh) + (dot(ah, bl) + dot(al, bh))


def inverse_of(block):
    i = lax.broadcasted_iota(jnp.int32, (B, B), 0)
    j = lax.broadcasted_iota(jnp.int32, (B, B), 1)
    diag = jnp.where(i == j, block, 0.0)
    two = jnp.where(i == j, 2.0, 0.0)
    across = 1.0 / jnp.sum(diag, axis=0, keepdims=True)
    down = 1.0 / jnp.sum(diag, axis=1, keepdims=True)
    first = down * (two - block * across)
    return mult(first, two - mult(block, first))


def kernel(m_ref, o_ref, tile, ubuf, wbuf, low0, uhigh, ulow, ssem, rsem, zssem, zrsem, lsem, osem, zready):
    r = lax.axis_index("row")
    z = lax.axis_index("col")
    y, x, c = r // (2 * NX), (r // 2) % NX, r % 2
    odd = x % 2
    other = x + 1 - 2 * odd
    side = jnp.where((x == 1) | (x == 2), 1, 0)
    idle = jnp.where(r == 0, 1, 0)
    busy = 1 - idle

    def at(yy, xx, cc, zz):
        return ((yy * NX + xx) * 2 + cc, zz)

    has_f1, y1 = lookup(y, branch(Y_TREE, 0))
    has_f2, y2 = lookup(y, branch(Y_TREE, 1))
    has_up, yup = lookup(y, parents(Y_TREE))
    source = jnp.where((y == 0) & (x < 2), 1, 0)
    far_in = jnp.where((y == 0) & (x >= 2), 1, 0)
    has_z1, z1 = lookup(z, branch(Z_TREE, 0))
    has_z2, z2 = lookup(z, branch(Z_TREE, 1))
    has_zup, zup = lookup(z, parents(Z_TREE))
    has_z1, has_z2, has_zup = has_z1 * busy, has_z2 * busy, has_zup * busy
    early, _ = lookup(z, {k: 0 for k in EARLY})
    early1, _ = lookup(z1, {k: 0 for k in EARLY})
    early2, _ = lookup(z2, {k: 0 for k in EARLY})
    early1, early2 = has_z1 * early1, has_z2 * early2
    late1, late2 = has_z1 - early1, has_z2 - early2
    xfar = NX - 1 - x
    ex_to = (jnp.where(r == 2, 1, (y * NX + other) * 2 + c), z)
    ex_got = jnp.where(r == 2, RSS, RX)
    straight = jnp.where((z == 0) & (r == 0), 1, 0)
    third = jnp.where((z == 0) & (c == 0) & (x == 2), 1, 0)
    has_ex = jnp.where((z == 0) & (c == 0) & (x == 3), 0, 1)
    has_sib = jnp.where(r == 1, 0, 1)

    mine = c + 2 * side
    theirs = c + 2 - 2 * side
    n_mine = jnp.where(mine == 3, LAST, NCH)
    n_theirs = jnp.where(theirs == 3, LAST, NCH)
    sib_p = 1 - c + 2 * side
    sib_s = 1 - c + 2 - 2 * side
    n_sib_p = jnp.where(sib_p == 3, LAST, NCH)
    n_sib_s = jnp.where(sib_s == 3, LAST, NCH)

    load = pltpu.make_async_copy(m_ref, tile, lsem.at[0])
    load.start()
    full = (source == 1) & (mine != 3)
    part = (source == 1) & (mine == 3)

    def own(n):
        return pltpu.make_async_copy(
            m_ref.at[pl.ds(0, n)], ubuf.at[pl.ds(pl.multiple_of(mine * ROWS, CH), n)], lsem.at[1]
        )

    @pl.when(full)
    def _():
        own(ROWS).start()

    @pl.when(part)
    def _():
        own(LAST * CH).start()

    bar = pltpu.get_barrier_semaphore()

    def hello(where):
        pl.semaphore_signal(bar, inc=1, device_id=where, device_id_type=MESH)

    @pl.when(has_up == 1)
    def _():
        hello(at(yup, x, c, z))

    @pl.when(far_in == 1)
    def _():
        hello(at(0, xfar, c, z))

    @pl.when((has_zup == 1) & (early == 1))
    def _():
        hello((r, zup))

    @pl.when(late1 == 1)
    def _():
        hello((r, z1))

    @pl.when(late2 == 1)
    def _():
        hello((r, z2))

    @pl.when(busy == 1)
    def _():
        hello(at(y, x, 1 - c, z))

    @pl.when((busy == 1) & (third == 0))
    def _():
        hello(at(y, other, c, z))

    @pl.when((third == 1) & (r == 4))
    def _():
        hello((0, z))

    @pl.when(r == 1)
    def _():
        hello((2, z))

    greeted = jnp.where((has_zup == 1) & (early == 0), 1, 0)
    pl.semaphore_wait(bar, has_ex + has_sib + straight + has_f1 + has_f2 + source + early1 + early2 + greeted)

    @pl.when(greeted == 1)
    def _():
        pl.semaphore_signal(zready, inc=1, device_id=(r, zup), device_id_type=MESH)

    def rows_of(block, i):
        return pl.ds(pl.multiple_of(block * ROWS + i * CH, CH), CH)

    def copy(p, block, i, kind, got, where, own=False):
        start, width = PARTS[p]
        ref = ubuf.at[rows_of(block, i), pl.ds(start, width)]
        return pltpu.make_async_remote_copy(
            src_ref=m_ref.at[rows_of(0, i), pl.ds(start, width)] if own else ref,
            dst_ref=ref,
            send_sem=ssem.at[p, kind, i],
            recv_sem=rsem.at[p, got, i],
            device_id=where,
            device_id_type=MESH,
        )

    sibling = at(y, x, 1 - c, z)
    sends = (
        (FAR, source, RP, at(0, xfar, c, z)),
        (F1, has_f1, RP, at(y1, x, c, z)),
        (F2, has_f2, RP, at(y2, x, c, z)),
        (FAR2, straight, RX, (4, z)),
        (EX, has_ex, ex_got, ex_to),
        (SIBP, has_sib, RSP, sibling),
    )

    onward = (
        (G1, third * has_f1, RX, at(y1, x, c, z)),
        (G2, third * has_f2, RX, at(y2, x, c, z)),
        (SIBS, has_sib, RSS, sibling),
    )

    def first(p):
        def issue(i, own):
            for kind, has, got, where in sends:

                @pl.when(has == 1)
                def _(kind=kind, got=got, where=where):
                    copy(p, mine, i, kind, got, where, own).start()

        def body(i, carry):
            @pl.when(source == 1)
            def _():
                issue(i, True)

            @pl.when(source == 0)
            def _():
                copy(p, mine, i, F1, RP, sibling).wait_recv()
                issue(i, False)

            return carry

        lax.fori_loop(0, n_mine, body, 0)

    def second(p):
        def body(i, carry):
            copy(p, theirs, i, EX, RX, sibling).wait_recv()

            for kind, has, got, where in onward:

                @pl.when(has == 1)
                def _(kind=kind, got=got, where=where):
                    copy(p, theirs, i, kind, got, where).start()

            return carry

        def got_p(i, carry):
            copy(p, sib_p, i, SIBP, RSP, sibling).wait_recv()
            return carry

        def got_s(i, carry):
            copy(p, sib_s, i, SIBS, RSS, sibling).wait_recv()
            return carry

        @pl.when(busy == 1)
        def _():
            lax.fori_loop(0, n_theirs, body, 0)
            lax.fori_loop(0, n_sib_p, got_p, 0)
            lax.fori_loop(0, n_sib_s, got_s, 0)

    def sent(p):
        def body_p(i, carry):
            for kind, has, got, where in sends:

                @pl.when(has == 1)
                def _(kind=kind, got=got, where=where):
                    copy(p, mine, i, kind, got, where).wait_send()

            return carry

        def body_s(i, carry):
            for kind, has, got, where in onward:

                @pl.when(has == 1)
                def _(kind=kind, got=got, where=where):
                    copy(p, theirs, i, kind, got, where).wait_send()

            return carry

        lax.fori_loop(0, n_mine, body_p, 0)

        @pl.when(busy == 1)
        def _():
            lax.fori_loop(0, n_theirs, body_s, 0)

    def wcopy(i, kind, where):
        ref = wbuf.at[pl.ds(pl.multiple_of(i * CZ, CZ), CZ)]
        return pltpu.make_async_remote_copy(
            src_ref=ref,
            dst_ref=ref,
            send_sem=zssem.at[kind, i],
            recv_sem=zrsem.at[i],
            device_id=where,
            device_id_type=MESH,
        )

    down = ((0, has_z1, (r, z1)), (1, has_z2, (r, z2)))

    def along(i, carry):
        @pl.when(has_zup == 1)
        def _():
            wcopy(i, 0, (r, z1)).wait_recv()

        for kind, has, where in down:

            @pl.when(has == 1)
            def _(kind=kind, where=where):
                wcopy(i, kind, where).start()

        return carry

    def pass_on():
        @pl.when(late1 + late2 > 0)
        def _():
            pl.semaphore_wait(zready, late1 + late2)

        lax.fori_loop(0, NCZ, along, 0)

    def along_sent(i, carry):
        for kind, has, where in down:

            @pl.when(has == 1)
            def _(kind=kind, where=where):
                wcopy(i, kind, where).wait_send()

        return carry

    def give(k):
        cols = pl.ds(k * B, B)
        return pltpu.make_async_copy(tile.at[:, cols], o_ref.at[:, cols], osem.at[k])

    row_id = r * ROWS + lax.broadcasted_iota(jnp.int32, (ROWS, B), 0)
    below0 = row_id >= B
    below1 = row_id >= 2 * B

    ahead = (z != 0) | (source == 1)
    pass_first = (z == PASS_FIRST) & (busy == 1)
    first(0)

    @pl.when(ahead)
    def _():
        first(1)

    pl.when(pass_first)(pass_on)
    second(0)
    load.wait()

    @pl.when(full)
    def _():
        own(ROWS).wait()

    @pl.when(part)
    def _():
        own(LAST * CH).wait()

    @pl.when((z == 0) & (busy == 1))
    def _():
        second0 = inverse_of(ubuf[:B, :B])
        s0 = split(second0)

        def times(a, pair):
            ah, al = split(a)
            return dot(ah, pair[0]) + (dot(ah, pair[1]) + dot(al, pair[0]))

        l10 = times(ubuf[B : 2 * B, :B], s0)
        lower0 = times(tile[:, :B], s0)
        u01 = split(ubuf[:B, B : 2 * B])
        block1 = ubuf[B : 2 * B, B : 2 * B] - times(l10, u01)
        panel1 = tile[:, B : 2 * B] - times(lower0, u01)
        lower1 = mult(panel1, inverse_of(block1))
        w0 = lower0 - mult(lower1, l10)
        wbuf[:, :B] = jnp.where(below1, w0, jnp.where(below0, lower0, 0.0))
        wbuf[:, B:] = jnp.where(below1, lower1, 0.0)
        low0[...] = lower0
        tile[:, B : 2 * B] = jnp.where(below1, lower1, jnp.where(below0, panel1, tile[:, B : 2 * B]))
        pass_on()

    @pl.when(jnp.logical_not(ahead))
    def _():
        first(1)

    second(1)

    @pl.when((z != 0) & (busy == 1))
    def _():
        def prepare():
            for start in range(0, COLS, B):
                uhigh[:, start : start + B], ulow[:, start : start + B] = split(ubuf[:, start : start + B])

        pl.when(has_z1 == 0)(prepare)
        pl.when(jnp.logical_not(pass_first))(pass_on)
        pl.when(has_z1 == 1)(prepare)
        wh, wl = split(wbuf[...])
        for k in range(COLS // B):
            uh, ul = uhigh[:, k * B : (k + 1) * B], ulow[:, k * B : (k + 1) * B]
            tile[:, k * B : (k + 1) * B] -= dot(wh, uh) + (dot(wh, ul) + dot(wl, uh))
            give(k).start()

    @pl.when((z == 0) & (busy == 1))
    def _():
        tile[:, 2 * B :] -= mult(wbuf[...], ubuf[:, 2 * B :])
        tile[:, :B] = jnp.where(below0, low0[...], tile[:, :B])

    @pl.when((z == 0) | (idle == 1))
    def _():
        for k in range(COLS // B):
            give(k).start()

    sent(0)
    sent(1)
    lax.fori_loop(0, NCZ, along_sent, 0)
    for k in range(COLS // B):
        give(k).wait()


def on_device(matrix):
    return pl.pallas_call(
        kernel,
        out_shape=jax.ShapeDtypeStruct((ROWS, COLS), jnp.float32),
        in_specs=[pl.BlockSpec(memory_space=pltpu.HBM)],
        out_specs=pl.BlockSpec(memory_space=pl.ANY),
        scratch_shapes=[
            pltpu.VMEM((ROWS, COLS), jnp.float32),
            pltpu.VMEM((2 * B, COLS), jnp.float32),
            pltpu.VMEM((ROWS, 2 * B), jnp.float32),
            pltpu.VMEM((ROWS, B), jnp.float32),
            pltpu.VMEM((2 * B, COLS), jnp.bfloat16),
            pltpu.VMEM((2 * B, COLS), jnp.bfloat16),
            pltpu.SemaphoreType.DMA((2, 9, NCH)),
            pltpu.SemaphoreType.DMA((2, 4, NCH)),
            pltpu.SemaphoreType.DMA((2, NCZ)),
            pltpu.SemaphoreType.DMA((NCZ,)),
            pltpu.SemaphoreType.DMA((2,)),
            pltpu.SemaphoreType.DMA((COLS // B,)),
            pltpu.SemaphoreType.REGULAR,
        ],
        compiler_params=pltpu.CompilerParams(
            collective_id=0, has_side_effects=True, vmem_limit_bytes=VMEM
        ),
        name="panel_steps",
    )(matrix)


def solution(mesh):
    return jax.shard_map(
        on_device,
        mesh=mesh,
        in_specs=(P("row", "col"),),
        out_specs=P("row", "col"),
        check_vma=False,
    )
```

```python
import jax
import jax.numpy as jnp
from jax import lax
from jax.experimental import pallas as pl
from jax.experimental.pallas import tpu as pltpu
from jax.sharding import PartitionSpec as P

B = 256
ROWS, COLS = 144, 768
NX, NY, NZ = 4, 8, 12
CH = 16
NCH = ROWS // CH
CZ = 8
NCZ = ROWS // CZ
LAST = (2 * B - 3 * ROWS) // CH
PARTS = ((0, 2 * B), (2 * B, COLS - 2 * B))
MESH = pl.DeviceIdType.MESH
VMEM = 54500 << 10
F1, F2, FAR, EX, SIBP, SIBS, FAR2, G1, G2 = range(9)
RP, RX = range(2)
SP, SS = range(2)

Y_TREE = {0: (2, 6), 2: (3, 1), 6: (5, 7), 3: (4, None)}
Z_TREE = {
    0: (1, 9),
    1: (2, None),
    2: (3, None),
    3: (4, None),
    9: (6, 10),
    10: (11, None),
    6: (5, 7),
    7: (8, None),
}
EARLY = (5, 6)
PASS_FIRST = 9


def lookup(value, table):
    found = jnp.int32(0)
    entry = jnp.int32(0)
    for key, item in table.items():
        found = jnp.where(value == key, 1, found)
        entry = jnp.where(value == key, item, entry)
    return found, entry


def branch(tree, which):
    return {k: v[which] for k, v in tree.items() if v[which] is not None}


def parents(tree):
    return {child: k for k, v in tree.items() for child in v if child is not None}


def split(v):
    high = v.astype(jnp.bfloat16)
    low = (v - high.astype(jnp.float32)).astype(jnp.bfloat16)
    return high, low


def dot(a, b):
    return jnp.dot(a, b, preferred_element_type=jnp.float32)


def mult(a, b):
    ah, al = split(a)
    bh, bl = split(b)
    return dot(ah, bh) + (dot(ah, bl) + dot(al, bh))


def inverse_of(block):
    i = lax.broadcasted_iota(jnp.int32, (B, B), 0)
    j = lax.broadcasted_iota(jnp.int32, (B, B), 1)
    diag = jnp.where(i == j, block, 0.0)
    two = jnp.where(i == j, 2.0, 0.0)
    across = 1.0 / jnp.sum(diag, axis=0, keepdims=True)
    down = 1.0 / jnp.sum(diag, axis=1, keepdims=True)
    first = down * (two - block * across)
    return mult(first, two - mult(block, first))


def kernel(m_ref, o_ref, tile, ubuf, wbuf, low0, uhigh, ulow, ssem, rsem, ysem, zssem, zrsem, lsem, osem, zready):
    r = lax.axis_index("row")
    z = lax.axis_index("col")
    y, x, c = r // (2 * NX), (r // 2) % NX, r % 2
    odd = x % 2
    other = x + 1 - 2 * odd
    side = jnp.where((x == 1) | (x == 2), 1, 0)
    idle = jnp.where(r == 0, 1, 0)
    busy = 1 - idle

    def at(yy, xx, cc, zz):
        return ((yy * NX + xx) * 2 + cc, zz)

    has_f1, y1 = lookup(y, branch(Y_TREE, 0))
    has_f2, y2 = lookup(y, branch(Y_TREE, 1))
    has_up, yup = lookup(y, parents(Y_TREE))
    source = jnp.where((y == 0) & (x < 2), 1, 0)
    far_in = jnp.where((y == 0) & (x >= 2), 1, 0)
    has_z1, z1 = lookup(z, branch(Z_TREE, 0))
    has_z2, z2 = lookup(z, branch(Z_TREE, 1))
    has_zup, zup = lookup(z, parents(Z_TREE))
    has_z1, has_z2, has_zup = has_z1 * busy, has_z2 * busy, has_zup * busy
    early, _ = lookup(z, {k: 0 for k in EARLY})
    early1, _ = lookup(z1, {k: 0 for k in EARLY})
    early2, _ = lookup(z2, {k: 0 for k in EARLY})
    early1, early2 = has_z1 * early1, has_z2 * early2
    late1, late2 = has_z1 - early1, has_z2 - early2
    xfar = NX - 1 - x
    straight = jnp.where((z == 0) & (r == 0), 1, 0)
    third = jnp.where((z == 0) & (c == 0) & (x == 2), 1, 0)
    has_ex = jnp.where((z == 0) & (c == 0) & (x == 3), 0, 1)
    has_sib = jnp.where(r == 1, 0, 1)

    mine = c + 2 * side
    theirs = c + 2 - 2 * side
    n_mine = jnp.where(mine == 3, LAST, NCH)
    n_theirs = jnp.where(theirs == 3, LAST, NCH)
    sib_p = 1 - c + 2 * side
    sib_s = 1 - c + 2 - 2 * side

    load = pltpu.make_async_copy(m_ref, tile, lsem.at[0])
    load.start()
    full = (source == 1) & (mine != 3)
    part = (source == 1) & (mine == 3)

    def own(n):
        return pltpu.make_async_copy(
            m_ref.at[pl.ds(0, n)], ubuf.at[pl.ds(pl.multiple_of(mine * ROWS, CH), n)], lsem.at[1]
        )

    @pl.when(full)
    def _():
        own(ROWS).start()

    @pl.when(part)
    def _():
        own(LAST * CH).start()

    bar = pltpu.get_barrier_semaphore()

    def hello(where):
        pl.semaphore_signal(bar, inc=1, device_id=where, device_id_type=MESH)

    @pl.when(has_up == 1)
    def _():
        hello(at(yup, x, c, z))

    @pl.when(far_in == 1)
    def _():
        hello(at(0, xfar, c, z))

    @pl.when((has_zup == 1) & (early == 1))
    def _():
        hello((r, zup))

    @pl.when(late1 == 1)
    def _():
        hello((r, z1))

    @pl.when(late2 == 1)
    def _():
        hello((r, z2))

    @pl.when(busy == 1)
    def _():
        hello(at(y, x, 1 - c, z))

    @pl.when((busy == 1) & (third == 0))
    def _():
        hello(at(y, other, c, z))

    @pl.when((third == 1) & (r == 4))
    def _():
        hello((0, z))

    @pl.when(r == 1)
    def _():
        hello((2, z))

    greeted = jnp.where((has_zup == 1) & (early == 0), 1, 0)
    pl.semaphore_wait(bar, has_ex + straight + has_sib + has_f1 + has_f2 + source + early1 + early2 + greeted)

    @pl.when(greeted == 1)
    def _():
        pl.semaphore_signal(zready, inc=1, device_id=(r, zup), device_id_type=MESH)

    def rows_of(block, i):
        return pl.ds(pl.multiple_of(block * ROWS + i * CH, CH), CH)

    def moved(p, rows, kind, recv, where, src=None):
        ref = ubuf.at[rows, pl.ds(*PARTS[p])]
        return pltpu.make_async_remote_copy(
            src_ref=ref if src is None else src,
            dst_ref=ref,
            send_sem=ssem.at[p, kind],
            recv_sem=recv,
            device_id=where,
            device_id_type=MESH,
        )

    def whole(p, block, act):
        def of(n):
            act(pl.ds(pl.multiple_of(block * ROWS, CH), n))

        pl.when(block != 3)(lambda: of(ROWS))
        pl.when(block == 3)(lambda: of(LAST * CH))

    sibling = at(y, x, 1 - c, z)
    sends = (
        (FAR, source, RP, at(0, xfar, c, z)),
        (FAR2, straight, RX, (4, z)),
        (F1, has_f1, RP, at(y1, x, c, z)),
        (F2, has_f2, RP, at(y2, x, c, z)),
    )
    ex_to = at(y, other, c, z)
    plain_ex = (has_ex == 1) & (r != 2) & (straight == 0)
    onward = (
        (G1, third * has_f1, at(y1, x, c, z)),
        (G2, third * has_f2, at(y2, x, c, z)),
    )

    def first(p):
        def issue(i, own):
            rows = rows_of(mine, i)
            src = m_ref.at[rows_of(0, i), pl.ds(*PARTS[p])] if own else None
            for kind, has, got, where in sends:

                @pl.when(has == 1)
                def _(kind=kind, got=got, where=where):
                    moved(p, rows, kind, rsem.at[p, got, i], where, src).start()

            @pl.when(plain_ex)
            def _():
                moved(p, rows, EX, rsem.at[p, RX, i], ex_to, src).start()

            @pl.when(r == 2)
            def _():
                moved(p, rows, EX, ysem.at[p, SS], (1, z), src).start()

            @pl.when(has_sib == 1)
            def _():
                moved(p, rows, SIBP, ysem.at[p, SP], sibling, src).start()

        def body(i, carry):
            @pl.when(source == 1)
            def _():
                issue(i, True)

            @pl.when(source == 0)
            def _():
                moved(p, rows_of(mine, i), F1, rsem.at[p, RP, i], sibling).wait_recv()
                issue(i, False)

            return carry

        lax.fori_loop(0, n_mine, body, 0)

        @pl.when(straight == 1)
        def _():
            def exchange(i, carry):
                src = m_ref.at[rows_of(0, i), pl.ds(*PARTS[p])]
                moved(p, rows_of(mine, i), EX, rsem.at[p, RX, i], ex_to, src).start()
                return carry

            lax.fori_loop(0, NCH, exchange, 0)

    def second(p):
        def body(i, carry):
            rows = rows_of(theirs, i)
            moved(p, rows, SIBS, rsem.at[p, RX, i], sibling).wait_recv()

            @pl.when(third == 1)
            def _():
                for kind, has, where in onward:

                    @pl.when(has == 1)
                    def _(kind=kind, where=where):
                        moved(p, rows, kind, rsem.at[p, RX, i], where).start()

            @pl.when(has_sib == 1)
            def _():
                moved(p, rows, SIBS, ysem.at[p, SS], sibling).start()

            return carry

        @pl.when(busy == 1)
        def _():
            lax.fori_loop(0, n_theirs, body, 0)
            whole(p, sib_p, lambda rows: moved(p, rows, SIBP, ysem.at[p, SP], sibling).wait_recv())
            whole(p, sib_s, lambda rows: moved(p, rows, SIBS, ysem.at[p, SS], sibling).wait_recv())

    def sent(p):
        def done(kind, block):
            whole(p, block, lambda rows: moved(p, rows, kind, rsem.at[p, RP, 0], sibling).wait_send())

        for kind, has, _, _ in sends:
            pl.when(has == 1)(lambda kind=kind: done(kind, mine))

        for kind, has, _ in onward:
            pl.when(has == 1)(lambda kind=kind: done(kind, theirs))

        pl.when(has_ex == 1)(lambda: done(EX, mine))
        pl.when(has_sib == 1)(lambda: done(SIBP, mine))
        pl.when((busy == 1) & (has_sib == 1))(lambda: done(SIBS, theirs))

    def wcopy(i, kind, where):
        ref = wbuf.at[pl.ds(pl.multiple_of(i * CZ, CZ), CZ)]
        return pltpu.make_async_remote_copy(
            src_ref=ref,
            dst_ref=ref,
            send_sem=zssem.at[kind],
            recv_sem=zrsem.at[i],
            device_id=where,
            device_id_type=MESH,
        )

    down = ((0, has_z1, (r, z1)), (1, has_z2, (r, z2)))

    def along(i, carry):
        @pl.when(has_zup == 1)
        def _():
            wcopy(i, 0, (r, z1)).wait_recv()

        for kind, has, where in down:

            @pl.when(has == 1)
            def _(kind=kind, where=where):
                wcopy(i, kind, where).start()

        return carry

    def pass_on():
        @pl.when(late1 + late2 > 0)
        def _():
            pl.semaphore_wait(zready, late1 + late2)

        lax.fori_loop(0, NCZ, along, 0)

    def passed():
        for kind, has, where in down:

            @pl.when(has == 1)
            def _(kind=kind, where=where):
                pltpu.make_async_remote_copy(
                    src_ref=wbuf,
                    dst_ref=wbuf,
                    send_sem=zssem.at[kind],
                    recv_sem=zrsem.at[0],
                    device_id=where,
                    device_id_type=MESH,
                ).wait_send()

    def give(k):
        cols = pl.ds(k * B, B)
        return pltpu.make_async_copy(tile.at[:, cols], o_ref.at[:, cols], osem.at[k])

    row_id = r * ROWS + lax.broadcasted_iota(jnp.int32, (ROWS, B), 0)
    below0 = row_id >= B
    below1 = row_id >= 2 * B

    ahead = (z != 0) | (source == 1)
    pass_first = (z == PASS_FIRST) & (busy == 1)
    first(0)

    @pl.when(ahead)
    def _():
        first(1)

    pl.when(pass_first)(pass_on)
    second(0)
    load.wait()

    @pl.when(full)
    def _():
        own(ROWS).wait()

    @pl.when(part)
    def _():
        own(LAST * CH).wait()

    @pl.when((z == 0) & (busy == 1))
    def _():
        second0 = inverse_of(ubuf[:B, :B])
        s0 = split(second0)

        def times(a, pair):
            ah, al = split(a)
            return dot(ah, pair[0]) + (dot(ah, pair[1]) + dot(al, pair[0]))

        l10 = times(ubuf[B : 2 * B, :B], s0)
        lower0 = times(tile[:, :B], s0)
        u01 = split(ubuf[:B, B : 2 * B])
        block1 = ubuf[B : 2 * B, B : 2 * B] - times(l10, u01)
        panel1 = tile[:, B : 2 * B] - times(lower0, u01)
        lower1 = mult(panel1, inverse_of(block1))
        w0 = lower0 - mult(lower1, l10)
        wbuf[:, :B] = jnp.where(below1, w0, jnp.where(below0, lower0, 0.0))
        wbuf[:, B:] = jnp.where(below1, lower1, 0.0)
        low0[...] = lower0
        tile[:, B : 2 * B] = jnp.where(below1, lower1, jnp.where(below0, panel1, tile[:, B : 2 * B]))
        pass_on()

    @pl.when(jnp.logical_not(ahead))
    def _():
        first(1)

    second(1)

    @pl.when((z != 0) & (busy == 1))
    def _():
        def prepare():
            for start in range(0, COLS, B):
                uhigh[:, start : start + B], ulow[:, start : start + B] = split(ubuf[:, start : start + B])

        pl.when(has_z1 == 0)(prepare)
        sent(0)
        sent(1)
        pl.when(jnp.logical_not(pass_first))(pass_on)
        pl.when(has_z1 == 1)(prepare)
        wh, wl = split(wbuf[...])
        for k in range(COLS // B):
            uh, ul = uhigh[:, k * B : (k + 1) * B], ulow[:, k * B : (k + 1) * B]
            tile[:, k * B : (k + 1) * B] -= dot(wh, uh) + (dot(wh, ul) + dot(wl, uh))
            give(k).start()

    @pl.when((z == 0) & (busy == 1))
    def _():
        tile[:, 2 * B :] -= mult(wbuf[...], ubuf[:, 2 * B :])
        tile[:, :B] = jnp.where(below0, low0[...], tile[:, :B])

    @pl.when((z == 0) | (idle == 1))
    def _():
        for k in range(COLS // B):
            give(k).start()

    @pl.when((z == 0) | (idle == 1))
    def _():
        sent(0)
        sent(1)

    passed()
    for k in range(COLS // B):
        give(k).wait()


def on_device(matrix):
    return pl.pallas_call(
        kernel,
        out_shape=jax.ShapeDtypeStruct((ROWS, COLS), jnp.float32),
        in_specs=[pl.BlockSpec(memory_space=pltpu.HBM)],
        out_specs=pl.BlockSpec(memory_space=pl.ANY),
        scratch_shapes=[
            pltpu.VMEM((ROWS, COLS), jnp.float32),
            pltpu.VMEM((2 * B, COLS), jnp.float32),
            pltpu.VMEM((ROWS, 2 * B), jnp.float32),
            pltpu.VMEM((ROWS, B), jnp.float32),
            pltpu.VMEM((2 * B, COLS), jnp.bfloat16),
            pltpu.VMEM((2 * B, COLS), jnp.bfloat16),
            pltpu.SemaphoreType.DMA((2, 9)),
            pltpu.SemaphoreType.DMA((2, 2, NCH)),
            pltpu.SemaphoreType.DMA((2, 2)),
            pltpu.SemaphoreType.DMA((2,)),
            pltpu.SemaphoreType.DMA((NCZ,)),
            pltpu.SemaphoreType.DMA((2,)),
            pltpu.SemaphoreType.DMA((COLS // B,)),
            pltpu.SemaphoreType.REGULAR,
        ],
        compiler_params=pltpu.CompilerParams(
            collective_id=0, has_side_effects=True, vmem_limit_bytes=VMEM
        ),
        name="panel_steps",
    )(matrix)


def solution(mesh):
    return jax.shard_map(
        on_device,
        mesh=mesh,
        in_specs=(P("row", "col"),),
        out_specs=P("row", "col"),
        check_vma=False,
    )
```

```python
import jax
import jax.numpy as jnp
from jax import lax
from jax.experimental import pallas as pl
from jax.experimental.pallas import tpu as pltpu
from jax.sharding import PartitionSpec as P

B = 256
ROWS, COLS = 144, 768
NX, NY, NZ = 4, 8, 12
CH = 16
NCH = ROWS // CH
CZ = 16
NCZ = ROWS // CZ
LAST = -(-(2 * B - 3 * ROWS) // CH)
PARTS = ((0, 2 * B), (2 * B, COLS - 2 * B))
MESH = pl.DeviceIdType.MESH
VMEM = 54500 << 10
F1, F2, FAR, EX, SIBP, SIBS, FAR2, G1, G2 = range(9)
RP, RX = range(2)
SP, SS = range(2)

Y_TREE = {0: (2, 6), 2: (3, 1), 6: (5, 7), 3: (4, None)}
Z_TREE = {
    0: (1, 9),
    1: (2, None),
    2: (3, None),
    3: (4, None),
    9: (6, 10),
    10: (11, None),
    6: (5, 7),
    7: (8, None),
}
HALF, HALF_FROM, HALF_PARENT = 8, 9, 7
EARLY = (5, 6)
PASS_FIRST = 9


def lookup(value, table):
    found = jnp.int32(0)
    entry = jnp.int32(0)
    for key, item in table.items():
        found = jnp.where(value == key, 1, found)
        entry = jnp.where(value == key, item, entry)
    return found, entry


def branch(tree, which):
    return {k: v[which] for k, v in tree.items() if v[which] is not None}


def parents(tree):
    return {child: k for k, v in tree.items() for child in v if child is not None}


def split(v):
    high = v.astype(jnp.bfloat16)
    low = (v - high.astype(jnp.float32)).astype(jnp.bfloat16)
    return high, low


def dot(a, b):
    return jnp.dot(a, b, preferred_element_type=jnp.float32)


def mult(a, b):
    ah, al = split(a)
    bh, bl = split(b)
    return dot(ah, bh) + (dot(ah, bl) + dot(al, bh))


def factors_of(block):
    i = lax.broadcasted_iota(jnp.int32, (B, B), 0)
    j = lax.broadcasted_iota(jnp.int32, (B, B), 1)
    diag = jnp.where(i == j, block, 0.0)
    two = jnp.where(i == j, 2.0, 0.0)
    across = 1.0 / jnp.sum(diag, axis=0, keepdims=True)
    down = 1.0 / jnp.sum(diag, axis=1, keepdims=True)
    return split(down * (two - block * across)), two


def times(a, pair):
    ah, al = split(a)
    return dot(ah, pair[0]) + (dot(ah, pair[1]) + dot(al, pair[0]))


def kernel(m_ref, o_ref, tile, ubuf, wbuf, low0, uhigh, ulow, ssem, rsem, ysem, zssem, zrsem, lsem, osem, zready):
    r = lax.axis_index("row")
    z = lax.axis_index("col")
    y, x, c = r // (2 * NX), (r // 2) % NX, r % 2
    odd = x % 2
    other = x + 1 - 2 * odd
    side = jnp.where((x == 1) | (x == 2), 1, 0)
    idle = jnp.where(r == 0, 1, 0)
    busy = 1 - idle

    def at(yy, xx, cc, zz):
        return ((yy * NX + xx) * 2 + cc, zz)

    has_f1, y1 = lookup(y, branch(Y_TREE, 0))
    has_f2, y2 = lookup(y, branch(Y_TREE, 1))
    has_up, yup = lookup(y, parents(Y_TREE))
    source = jnp.where((y == 0) & (x < 2), 1, 0)
    far_in = jnp.where((y == 0) & (x >= 2), 1, 0)
    has_z1, z1 = lookup(z, branch(Z_TREE, 0))
    has_z2, z2 = lookup(z, branch(Z_TREE, 1))
    has_zup, zup = lookup(z, parents(Z_TREE))
    has_z1, has_z2, has_zup = has_z1 * busy, has_z2 * busy, has_zup * busy
    early, _ = lookup(z, {k: 0 for k in EARLY})
    early1, _ = lookup(z1, {k: 0 for k in EARLY})
    early2, _ = lookup(z2, {k: 0 for k in EARLY})
    early1, early2 = has_z1 * early1, has_z2 * early2
    late1, late2 = has_z1 - early1, has_z2 - early2
    gives_half = jnp.where(z == HALF_FROM, busy, 0)
    xfar = NX - 1 - x
    straight = jnp.where((z == 0) & (r == 0), 1, 0)
    third = jnp.where((z == 0) & (c == 0) & (x == 2), 1, 0)
    has_ex = jnp.where((z == 0) & (c == 0) & (x == 3), 0, 1)
    has_sib = jnp.where(r == 1, 0, 1)

    mine = c + 2 * side
    theirs = c + 2 - 2 * side
    n_mine = jnp.where(mine == 3, LAST, NCH)
    n_theirs = jnp.where(theirs == 3, LAST, NCH)
    sib_p = 1 - c + 2 * side
    sib_s = 1 - c + 2 - 2 * side

    load = pltpu.make_async_copy(m_ref, tile, lsem.at[0])
    load.start()
    full = (source == 1) & (mine != 3)
    part = (source == 1) & (mine == 3)

    def own(n):
        return pltpu.make_async_copy(
            m_ref.at[pl.ds(0, n)], ubuf.at[pl.ds(pl.multiple_of(mine * ROWS, 8), n)], lsem.at[1]
        )

    @pl.when(full)
    def _():
        own(ROWS).start()

    @pl.when(part)
    def _():
        own(LAST * CH).start()

    bar = pltpu.get_barrier_semaphore()

    def hello(where):
        pl.semaphore_signal(bar, inc=1, device_id=where, device_id_type=MESH)

    @pl.when(has_up == 1)
    def _():
        hello(at(yup, x, c, z))

    @pl.when(far_in == 1)
    def _():
        hello(at(0, xfar, c, z))

    @pl.when((has_zup == 1) & (early == 1))
    def _():
        hello((r, zup))

    @pl.when((z == HALF) & (busy == 1))
    def _():
        hello((r, HALF_FROM))

    @pl.when(late1 == 1)
    def _():
        hello((r, z1))

    @pl.when(late2 == 1)
    def _():
        hello((r, z2))

    @pl.when(busy == 1)
    def _():
        hello(at(y, x, 1 - c, z))

    @pl.when((busy == 1) & (third == 0))
    def _():
        hello(at(y, other, c, z))

    @pl.when((third == 1) & (r == 4))
    def _():
        hello((0, z))

    @pl.when(r == 1)
    def _():
        hello((2, z))

    greeted = jnp.where((has_zup == 1) & (early == 0), 1, 0)
    pl.semaphore_wait(bar, has_ex + straight + has_sib + has_f1 + has_f2 + source + early1 + early2 + gives_half + greeted)

    @pl.when(greeted == 1)
    def _():
        pl.semaphore_signal(zready, inc=1, device_id=(r, zup), device_id_type=MESH)

    def rows_of(block, i):
        return pl.ds(pl.multiple_of(block * ROWS + i * CH, 8), CH)

    def moved(p, rows, kind, recv, where, src=None):
        ref = ubuf.at[rows, pl.ds(*PARTS[p])]
        return pltpu.make_async_remote_copy(
            src_ref=ref if src is None else src,
            dst_ref=ref,
            send_sem=ssem.at[p, kind],
            recv_sem=recv,
            device_id=where,
            device_id_type=MESH,
        )

    def whole(p, block, act):
        def of(n):
            act(pl.ds(pl.multiple_of(block * ROWS, 8), n))

        pl.when(block != 3)(lambda: of(ROWS))
        pl.when(block == 3)(lambda: of(LAST * CH))

    sibling = at(y, x, 1 - c, z)
    sends = (
        (FAR, source, RP, at(0, xfar, c, z)),
        (FAR2, straight, RX, (4, z)),
        (F1, has_f1, RP, at(y1, x, c, z)),
        (F2, has_f2, RP, at(y2, x, c, z)),
    )
    ex_to = at(y, other, c, z)
    plain_ex = (has_ex == 1) & (r != 2) & (straight == 0)
    onward = (
        (G1, third * has_f1, at(y1, x, c, z)),
        (G2, third * has_f2, at(y2, x, c, z)),
    )

    def first(p):
        def issue(i, own):
            rows = rows_of(mine, i)
            src = m_ref.at[rows_of(0, i), pl.ds(*PARTS[p])] if own else None
            for kind, has, got, where in sends:

                @pl.when(has == 1)
                def _(kind=kind, got=got, where=where):
                    moved(p, rows, kind, rsem.at[p, got, i], where, src).start()

            @pl.when(plain_ex)
            def _():
                moved(p, rows, EX, rsem.at[p, RX, i], ex_to, src).start()

            @pl.when(r == 2)
            def _():
                moved(p, rows, EX, ysem.at[p, SS], (1, z), src).start()

            @pl.when(has_sib == 1)
            def _():
                moved(p, rows, SIBP, ysem.at[p, SP], sibling, src).start()

        def body(i, carry):
            @pl.when(source == 1)
            def _():
                issue(i, True)

            @pl.when(source == 0)
            def _():
                moved(p, rows_of(mine, i), F1, rsem.at[p, RP, i], sibling).wait_recv()
                issue(i, False)

            return carry

        lax.fori_loop(0, n_mine, body, 0)

        @pl.when(straight == 1)
        def _():
            def exchange(i, carry):
                src = m_ref.at[rows_of(0, i), pl.ds(*PARTS[p])]
                moved(p, rows_of(mine, i), EX, rsem.at[p, RX, i], ex_to, src).start()
                return carry

            lax.fori_loop(0, NCH, exchange, 0)

    def second(p):
        def body(i, carry):
            rows = rows_of(theirs, i)
            moved(p, rows, SIBS, rsem.at[p, RX, i], sibling).wait_recv()

            @pl.when(third == 1)
            def _():
                for kind, has, where in onward:

                    @pl.when(has == 1)
                    def _(kind=kind, where=where):
                        moved(p, rows, kind, rsem.at[p, RX, i], where).start()

            @pl.when(has_sib == 1)
            def _():
                moved(p, rows, SIBS, ysem.at[p, SS], sibling).start()

            return carry

        @pl.when(busy == 1)
        def _():
            lax.fori_loop(0, n_theirs, body, 0)
            whole(p, sib_p, lambda rows: moved(p, rows, SIBP, ysem.at[p, SP], sibling).wait_recv())
            whole(p, sib_s, lambda rows: moved(p, rows, SIBS, ysem.at[p, SS], sibling).wait_recv())

    def sent(p):
        def done(kind, block):
            whole(p, block, lambda rows: moved(p, rows, kind, rsem.at[p, RP, 0], sibling).wait_send())

        for kind, has, _, _ in sends:
            pl.when(has == 1)(lambda kind=kind: done(kind, mine))

        for kind, has, _ in onward:
            pl.when(has == 1)(lambda kind=kind: done(kind, theirs))

        pl.when(has_ex == 1)(lambda: done(EX, mine))
        pl.when(has_sib == 1)(lambda: done(SIBP, mine))
        pl.when((busy == 1) & (has_sib == 1))(lambda: done(SIBS, theirs))

    def wcopy(h, i, kind, where):
        ref = wbuf.at[h, pl.ds(pl.multiple_of(i * CZ, CZ), CZ)]
        return pltpu.make_async_remote_copy(
            src_ref=ref,
            dst_ref=ref,
            send_sem=zssem.at[kind],
            recv_sem=zrsem.at[h, i],
            device_id=where,
            device_id_type=MESH,
        )

    down = ((0, has_z1, (r, z1)), (1, has_z2, (r, z2)))

    def along(h):
        def body(i, carry):
            @pl.when(has_zup == 1)
            def _():
                wcopy(h, i, 0, (r, z1)).wait_recv()

            for kind, has, where in down:

                @pl.when(has == 1 if h == 1 else (has == 1) & (z != HALF_PARENT))
                def _(kind=kind, where=where):
                    wcopy(h, i, kind, where).start()

            return carry

        lax.fori_loop(0, NCZ, body, 0)

    def children():
        @pl.when(late1 + late2 > 0)
        def _():
            pl.semaphore_wait(zready, late1 + late2)

    def pass_on():
        children()
        along(1)
        along(0)

        @pl.when(gives_half == 1)
        def _():
            def body(i, carry):
                wcopy(0, i, 2, (r, HALF)).start()
                return carry

            lax.fori_loop(0, NCZ, body, 0)

    def passed():
        def gone(ref, kind):
            pltpu.make_async_remote_copy(
                src_ref=ref,
                dst_ref=ref,
                send_sem=zssem.at[kind],
                recv_sem=zrsem.at[0, 0],
                device_id=(r, z1),
                device_id_type=MESH,
            ).wait_send()

        pl.when((has_z1 == 1) & (z == HALF_PARENT))(lambda: gone(wbuf.at[1], 0))
        pl.when((has_z1 == 1) & (z != HALF_PARENT))(lambda: gone(wbuf, 0))
        pl.when(has_z2 == 1)(lambda: gone(wbuf, 1))
        pl.when(gives_half == 1)(lambda: gone(wbuf.at[0], 2))

    def give(k):
        cols = pl.ds(k * B, B)
        return pltpu.make_async_copy(tile.at[:, cols], o_ref.at[:, cols], osem.at[k])

    row_id = r * ROWS + lax.broadcasted_iota(jnp.int32, (ROWS, B), 0)
    below0 = row_id >= B
    below1 = row_id >= 2 * B

    ahead = (z != 0) | (source == 1)
    pass_first = (z == PASS_FIRST) & (busy == 1)
    first(0)

    pl.when(pass_first)(pass_on)

    @pl.when(ahead)
    def _():
        first(1)

    second(0)
    load.wait()

    @pl.when(full)
    def _():
        own(ROWS).wait()

    @pl.when(part)
    def _():
        own(LAST * CH).wait()

    @pl.when((z == 0) & (busy == 1))
    def _():
        first0, two = factors_of(ubuf[:B, :B])
        rest0 = split(two - times(ubuf[:B, :B], first0))
        l10 = times(times(ubuf[B : 2 * B, :B], first0), rest0)
        lower0 = times(times(tile[:, :B], first0), rest0)
        u01 = split(ubuf[:B, B : 2 * B])
        block1 = ubuf[B : 2 * B, B : 2 * B] - times(l10, u01)
        panel1 = tile[:, B : 2 * B] - times(lower0, u01)
        first1, _ = factors_of(block1)
        rest1 = split(two - times(block1, first1))
        lower1 = times(times(panel1, first1), rest1)
        wbuf[1] = jnp.where(below1, lower1, 0.0)
        children()
        along(1)
        w0 = lower0 - mult(lower1, l10)
        wbuf[0] = jnp.where(below1, w0, jnp.where(below0, lower0, 0.0))
        along(0)
        low0[...] = lower0
        tile[:, B : 2 * B] = jnp.where(below1, lower1, jnp.where(below0, panel1, tile[:, B : 2 * B]))

    @pl.when(jnp.logical_not(ahead))
    def _():
        first(1)

    second(1)

    def prepare():
        for start in range(0, COLS, B):
            uhigh[:, start : start + B], ulow[:, start : start + B] = split(ubuf[: 2 * B, start : start + B])

    def update(h):
        wh, wl = split(wbuf[h])
        for k in range(COLS // B):
            uh, ul = (u[h * B : (h + 1) * B, k * B : (k + 1) * B] for u in (uhigh, ulow))
            tile[:, k * B : (k + 1) * B] -= dot(wh, uh) + (dot(wh, ul) + dot(wl, uh))
            if h == 0:
                give(k).start()

    @pl.when((z != 0) & (busy == 1) & (has_z1 == 1))
    def _():
        sent(0)
        sent(1)
        pl.when(jnp.logical_not(pass_first))(pass_on)
        prepare()
        update(1)
        update(0)

    @pl.when((z != 0) & (busy == 1) & (has_z1 == 0))
    def _():
        prepare()
        sent(0)
        sent(1)
        along(1)
        update(1)
        along(0)
        update(0)

    @pl.when((z == 0) & (busy == 1))
    def _():
        for h in range(2):
            tile[:, 2 * B :] -= mult(wbuf[h], ubuf[h * B : (h + 1) * B, 2 * B :])

        tile[:, :B] = jnp.where(below0, low0[...], tile[:, :B])

    @pl.when((z == 0) | (idle == 1))
    def _():
        for k in range(COLS // B):
            give(k).start()

    @pl.when((z == 0) | (idle == 1))
    def _():
        sent(0)
        sent(1)

    passed()
    for k in range(COLS // B):
        give(k).wait()


def on_device(matrix):
    return pl.pallas_call(
        kernel,
        out_shape=jax.ShapeDtypeStruct((ROWS, COLS), jnp.float32),
        in_specs=[pl.BlockSpec(memory_space=pltpu.HBM)],
        out_specs=pl.BlockSpec(memory_space=pl.ANY),
        scratch_shapes=[
            pltpu.VMEM((ROWS, COLS), jnp.float32),
            pltpu.VMEM((3 * ROWS + LAST * CH, COLS), jnp.float32),
            pltpu.VMEM((2, ROWS, B), jnp.float32),
            pltpu.VMEM((ROWS, B), jnp.float32),
            pltpu.VMEM((2 * B, COLS), jnp.bfloat16),
            pltpu.VMEM((2 * B, COLS), jnp.bfloat16),
            pltpu.SemaphoreType.DMA((2, 9)),
            pltpu.SemaphoreType.DMA((2, 2, NCH)),
            pltpu.SemaphoreType.DMA((2, 2)),
            pltpu.SemaphoreType.DMA((3,)),
            pltpu.SemaphoreType.DMA((2, NCZ)),
            pltpu.SemaphoreType.DMA((2,)),
            pltpu.SemaphoreType.DMA((COLS // B,)),
            pltpu.SemaphoreType.REGULAR,
        ],
        compiler_params=pltpu.CompilerParams(
            collective_id=0, has_side_effects=True, vmem_limit_bytes=VMEM
        ),
        name="panel_steps",
    )(matrix)


def solution(mesh):
    return jax.shard_map(
        on_device,
        mesh=mesh,
        in_specs=(P("row", "col"),),
        out_specs=P("row", "col"),
        check_vma=False,
    )
```

```python
import jax
import jax.numpy as jnp
from jax import lax
from jax.experimental import pallas as pl
from jax.experimental.pallas import tpu as pltpu
from jax.sharding import PartitionSpec as P

B = 256
ROWS, COLS = 144, 768
NX, NY, NZ = 4, 8, 12
CH = 8
NCH = ROWS // CH
CZ = 16
NCZ = ROWS // CZ
LAST = -(-(2 * B - 3 * ROWS) // CH)
PARTS = ((0, 2 * B), (2 * B, COLS - 2 * B))
MESH = pl.DeviceIdType.MESH
VMEM = 54500 << 10
F1, F2, FAR, EX, SIBP, SIBS, FAR2, G1, G2 = range(9)
RP, RX = range(2)
SP, SS = range(2)

Y_TREE = {0: (2, 6), 2: (3, 1), 6: (5, 7), 3: (4, None)}
Z_TREE = {
    0: (1, 9),
    1: (2, None),
    2: (3, None),
    3: (4, None),
    9: (6, 10),
    10: (11, None),
    6: (5, 7),
    7: (8, None),
}
HALF, HALF_FROM, HALF_PARENT = 8, 9, 7
EARLY = (5, 6)
PASS_FIRST = 9


def lookup(value, table):
    found = jnp.int32(0)
    entry = jnp.int32(0)
    for key, item in table.items():
        found = jnp.where(value == key, 1, found)
        entry = jnp.where(value == key, item, entry)
    return found, entry


def branch(tree, which):
    return {k: v[which] for k, v in tree.items() if v[which] is not None}


def parents(tree):
    return {child: k for k, v in tree.items() for child in v if child is not None}


def split(v):
    high = v.astype(jnp.bfloat16)
    low = (v - high.astype(jnp.float32)).astype(jnp.bfloat16)
    return high, low


def dot(a, b):
    return jnp.dot(a, b, preferred_element_type=jnp.float32)


def mult(a, b):
    ah, al = split(a)
    bh, bl = split(b)
    return dot(ah, bh) + (dot(ah, bl) + dot(al, bh))


def factors_of(block):
    i = lax.broadcasted_iota(jnp.int32, (B, B), 0)
    j = lax.broadcasted_iota(jnp.int32, (B, B), 1)
    diag = jnp.where(i == j, block, 0.0)
    two = jnp.where(i == j, 2.0, 0.0)
    across = 1.0 / jnp.sum(diag, axis=0, keepdims=True)
    down = 1.0 / jnp.sum(diag, axis=1, keepdims=True)
    return split(down * (two - block * across)), two


def times(a, pair):
    ah, al = split(a)
    return dot(ah, pair[0]) + (dot(ah, pair[1]) + dot(al, pair[0]))


def kernel(m_ref, o_ref, tile, ubuf, wbuf, low0, uhigh, ulow, ssem, rsem, ysem, zssem, zrsem, lsem, osem, zready):
    r = lax.axis_index("row")
    z = lax.axis_index("col")
    y, x, c = r // (2 * NX), (r // 2) % NX, r % 2
    odd = x % 2
    other = x + 1 - 2 * odd
    side = jnp.where((x == 1) | (x == 2), 1, 0)
    idle = jnp.where(r == 0, 1, 0)
    busy = 1 - idle

    def at(yy, xx, cc, zz):
        return ((yy * NX + xx) * 2 + cc, zz)

    has_f1, y1 = lookup(y, branch(Y_TREE, 0))
    has_f2, y2 = lookup(y, branch(Y_TREE, 1))
    has_up, yup = lookup(y, parents(Y_TREE))
    source = jnp.where((y == 0) & (x < 2), 1, 0)
    far_in = jnp.where((y == 0) & (x >= 2), 1, 0)
    has_z1, z1 = lookup(z, branch(Z_TREE, 0))
    has_z2, z2 = lookup(z, branch(Z_TREE, 1))
    has_zup, zup = lookup(z, parents(Z_TREE))
    has_z1, has_z2, has_zup = has_z1 * busy, has_z2 * busy, has_zup * busy
    early, _ = lookup(z, {k: 0 for k in EARLY})
    early1, _ = lookup(z1, {k: 0 for k in EARLY})
    early2, _ = lookup(z2, {k: 0 for k in EARLY})
    early1, early2 = has_z1 * early1, has_z2 * early2
    late1, late2 = has_z1 - early1, has_z2 - early2
    gives_half = jnp.where(z == HALF_FROM, busy, 0)
    xfar = NX - 1 - x
    straight = jnp.where((z == 0) & (r == 0), 1, 0)
    third = jnp.where((z == 0) & (c == 0) & (x == 2), 1, 0)
    has_ex = jnp.where((z == 0) & (c == 0) & (x == 3), 0, 1)
    has_sib = jnp.where(r == 1, 0, 1)

    mine = c + 2 * side
    theirs = c + 2 - 2 * side
    n_mine = jnp.where(mine == 3, LAST, NCH)
    n_theirs = jnp.where(theirs == 3, LAST, NCH)
    sib_p = 1 - c + 2 * side
    sib_s = 1 - c + 2 - 2 * side

    load = pltpu.make_async_copy(m_ref, tile, lsem.at[0])
    load.start()
    full = (source == 1) & (mine != 3)
    part = (source == 1) & (mine == 3)

    def own(n):
        return pltpu.make_async_copy(
            m_ref.at[pl.ds(0, n)], ubuf.at[pl.ds(pl.multiple_of(mine * ROWS, 8), n)], lsem.at[1]
        )

    @pl.when(full)
    def _():
        own(ROWS).start()

    @pl.when(part)
    def _():
        own(LAST * CH).start()

    bar = pltpu.get_barrier_semaphore()

    def hello(where):
        pl.semaphore_signal(bar, inc=1, device_id=where, device_id_type=MESH)

    @pl.when(has_up == 1)
    def _():
        hello(at(yup, x, c, z))

    @pl.when(far_in == 1)
    def _():
        hello(at(0, xfar, c, z))

    @pl.when((has_zup == 1) & (early == 1))
    def _():
        hello((r, zup))

    @pl.when((z == HALF) & (busy == 1))
    def _():
        hello((r, HALF_FROM))

    @pl.when(late1 == 1)
    def _():
        hello((r, z1))

    @pl.when(late2 == 1)
    def _():
        hello((r, z2))

    @pl.when(busy == 1)
    def _():
        hello(at(y, x, 1 - c, z))

    @pl.when((busy == 1) & (third == 0))
    def _():
        hello(at(y, other, c, z))

    @pl.when((third == 1) & (r == 4))
    def _():
        hello((0, z))

    @pl.when(r == 1)
    def _():
        hello((2, z))

    greeted = jnp.where((has_zup == 1) & (early == 0), 1, 0)
    pl.semaphore_wait(bar, has_ex + straight + has_sib + has_f1 + has_f2 + source + early1 + early2 + gives_half + greeted)

    @pl.when(greeted == 1)
    def _():
        pl.semaphore_signal(zready, inc=1, device_id=(r, zup), device_id_type=MESH)

    def rows_of(block, i):
        return pl.ds(pl.multiple_of(block * ROWS + i * CH, 8), CH)

    def moved(p, rows, kind, recv, where, src=None):
        ref = ubuf.at[rows, pl.ds(*PARTS[p])]
        return pltpu.make_async_remote_copy(
            src_ref=ref if src is None else src,
            dst_ref=ref,
            send_sem=ssem.at[p, kind],
            recv_sem=recv,
            device_id=where,
            device_id_type=MESH,
        )

    def whole(p, block, act):
        def of(n):
            act(pl.ds(pl.multiple_of(block * ROWS, 8), n))

        pl.when(block != 3)(lambda: of(ROWS))
        pl.when(block == 3)(lambda: of(LAST * CH))

    sibling = at(y, x, 1 - c, z)
    sends = (
        (F1, has_f1, RP, at(y1, x, c, z)),
        (F2, has_f2, RP, at(y2, x, c, z)),
        (FAR, source, RP, at(0, xfar, c, z)),
        (FAR2, straight, RX, (4, z)),
    )
    ex_to = at(y, other, c, z)
    plain_ex = (has_ex == 1) & (r != 2) & (straight == 0)
    onward = (
        (G1, third * has_f1, at(y1, x, c, z)),
        (G2, third * has_f2, at(y2, x, c, z)),
    )

    def first(p):
        def issue(i, own):
            rows = rows_of(mine, i)
            src = m_ref.at[rows_of(0, i), pl.ds(*PARTS[p])] if own else None
            for kind, has, got, where in sends if own else sends[:2]:

                @pl.when(has == 1)
                def _(kind=kind, got=got, where=where):
                    moved(p, rows, kind, rsem.at[p, got, i], where, src).start()

            @pl.when(plain_ex if own else has_ex == 1)
            def _():
                moved(p, rows, EX, rsem.at[p, RX, i], ex_to, src).start()

            if not own:
                moved(p, rows, SIBP, ysem.at[p, SP], sibling).start()
                return

            @pl.when(r == 2)
            def _():
                moved(p, rows, EX, ysem.at[p, SS], (1, z), src).start()

            @pl.when(has_sib == 1)
            def _():
                moved(p, rows, SIBP, ysem.at[p, SP], sibling, src).start()

        def body(i, carry):
            @pl.when(source == 1)
            def _():
                issue(i, True)

            @pl.when(source == 0)
            def _():
                moved(p, rows_of(mine, i), F1, rsem.at[p, RP, i], sibling).wait_recv()
                issue(i, False)

            return carry

        lax.fori_loop(0, n_mine, body, 0)

        @pl.when(straight == 1)
        def _():
            def exchange(i, carry):
                src = m_ref.at[rows_of(0, i), pl.ds(*PARTS[p])]
                moved(p, rows_of(mine, i), EX, rsem.at[p, RX, i], ex_to, src).start()
                return carry

            lax.fori_loop(0, NCH, exchange, 0)

    def second(p):
        def body(i, carry):
            rows = rows_of(theirs, i)
            moved(p, rows, SIBS, rsem.at[p, RX, i], sibling).wait_recv()

            @pl.when(third == 1)
            def _():
                for kind, has, where in onward:

                    @pl.when(has == 1)
                    def _(kind=kind, where=where):
                        moved(p, rows, kind, rsem.at[p, RX, i], where).start()

            @pl.when(has_sib == 1)
            def _():
                moved(p, rows, SIBS, ysem.at[p, SS], sibling).start()

            return carry

        @pl.when(busy == 1)
        def _():
            lax.fori_loop(0, n_theirs, body, 0)
            whole(p, sib_p, lambda rows: moved(p, rows, SIBP, ysem.at[p, SP], sibling).wait_recv())
            whole(p, sib_s, lambda rows: moved(p, rows, SIBS, ysem.at[p, SS], sibling).wait_recv())

    def sent(p):
        def done(kind, block):
            whole(p, block, lambda rows: moved(p, rows, kind, rsem.at[p, RP, 0], sibling).wait_send())

        for kind, has, _, _ in sends:
            pl.when(has == 1)(lambda kind=kind: done(kind, mine))

        for kind, has, _ in onward:
            pl.when(has == 1)(lambda kind=kind: done(kind, theirs))

        pl.when(has_ex == 1)(lambda: done(EX, mine))
        pl.when(has_sib == 1)(lambda: done(SIBP, mine))
        pl.when((busy == 1) & (has_sib == 1))(lambda: done(SIBS, theirs))

    def wcopy(h, i, kind, where):
        ref = wbuf.at[h, pl.ds(pl.multiple_of(i * CZ, CZ), CZ)]
        return pltpu.make_async_remote_copy(
            src_ref=ref,
            dst_ref=ref,
            send_sem=zssem.at[kind],
            recv_sem=zrsem.at[h, i],
            device_id=where,
            device_id_type=MESH,
        )

    down = ((0, has_z1, (r, z1)), (1, has_z2, (r, z2)))

    def along(h):
        def body(i, carry):
            @pl.when(has_zup == 1)
            def _():
                wcopy(h, i, 0, (r, z1)).wait_recv()

            for kind, has, where in down:

                @pl.when(has == 1 if h == 1 else (has == 1) & (z != HALF_PARENT))
                def _(kind=kind, where=where):
                    wcopy(h, i, kind, where).start()

            return carry

        lax.fori_loop(0, NCZ, body, 0)

    def children():
        @pl.when(late1 + late2 > 0)
        def _():
            pl.semaphore_wait(zready, late1 + late2)

    def pass_on():
        children()
        along(1)
        along(0)

        @pl.when(gives_half == 1)
        def _():
            def body(i, carry):
                wcopy(0, i, 2, (r, HALF)).start()
                return carry

            lax.fori_loop(0, NCZ, body, 0)

    def passed():
        def gone(ref, kind):
            pltpu.make_async_remote_copy(
                src_ref=ref,
                dst_ref=ref,
                send_sem=zssem.at[kind],
                recv_sem=zrsem.at[0, 0],
                device_id=(r, z1),
                device_id_type=MESH,
            ).wait_send()

        pl.when((has_z1 == 1) & (z == HALF_PARENT))(lambda: gone(wbuf.at[1], 0))
        pl.when((has_z1 == 1) & (z != HALF_PARENT))(lambda: gone(wbuf, 0))
        pl.when(has_z2 == 1)(lambda: gone(wbuf, 1))
        pl.when(gives_half == 1)(lambda: gone(wbuf.at[0], 2))

    def give(k):
        cols = pl.ds(k * B, B)
        return pltpu.make_async_copy(tile.at[:, cols], o_ref.at[:, cols], osem.at[k])

    row_id = r * ROWS + lax.broadcasted_iota(jnp.int32, (ROWS, B), 0)
    below0 = row_id >= B
    below1 = row_id >= 2 * B

    ahead = (z != 0) | (source == 1)
    pass_first = (z == PASS_FIRST) & (busy == 1)
    first(0)

    pl.when(pass_first)(pass_on)

    @pl.when(ahead)
    def _():
        first(1)

    second(0)
    load.wait()

    @pl.when(full)
    def _():
        own(ROWS).wait()

    @pl.when(part)
    def _():
        own(LAST * CH).wait()

    @pl.when((z == 0) & (busy == 1))
    def _():
        first0, two = factors_of(ubuf[:B, :B])
        rest0 = split(two - times(ubuf[:B, :B], first0))
        l10 = times(times(ubuf[B : 2 * B, :B], first0), rest0)
        lower0 = times(times(tile[:, :B], first0), rest0)
        u01 = split(ubuf[:B, B : 2 * B])
        block1 = ubuf[B : 2 * B, B : 2 * B] - times(l10, u01)
        panel1 = tile[:, B : 2 * B] - times(lower0, u01)
        first1, _ = factors_of(block1)
        rest1 = split(two - times(block1, first1))
        lower1 = times(times(panel1, first1), rest1)
        wbuf[1] = jnp.where(below1, lower1, 0.0)
        children()
        along(1)
        w0 = lower0 - mult(lower1, l10)
        wbuf[0] = jnp.where(below1, w0, jnp.where(below0, lower0, 0.0))
        along(0)
        low0[...] = lower0
        tile[:, B : 2 * B] = jnp.where(below1, lower1, jnp.where(below0, panel1, tile[:, B : 2 * B]))

    @pl.when(jnp.logical_not(ahead))
    def _():
        first(1)

    second(1)

    def prepare():
        for start in range(0, COLS, B):
            uhigh[:, start : start + B], ulow[:, start : start + B] = split(ubuf[: 2 * B, start : start + B])

    def update(h):
        wh, wl = split(wbuf[h])
        for k in range(COLS // B):
            uh, ul = (u[h * B : (h + 1) * B, k * B : (k + 1) * B] for u in (uhigh, ulow))
            tile[:, k * B : (k + 1) * B] -= dot(wh, uh) + (dot(wh, ul) + dot(wl, uh))
            if h == 0:
                give(k).start()

    @pl.when((z != 0) & (busy == 1) & (has_z1 == 1))
    def _():
        sent(0)
        sent(1)
        pl.when(jnp.logical_not(pass_first))(pass_on)
        prepare()
        update(1)
        update(0)

    @pl.when((z != 0) & (busy == 1) & (has_z1 == 0))
    def _():
        prepare()
        sent(0)
        sent(1)
        along(1)
        update(1)
        along(0)
        update(0)

    @pl.when((z == 0) & (busy == 1))
    def _():
        for h in range(2):
            tile[:, 2 * B :] -= mult(wbuf[h], ubuf[h * B : (h + 1) * B, 2 * B :])

        tile[:, :B] = jnp.where(below0, low0[...], tile[:, :B])

    @pl.when((z == 0) | (idle == 1))
    def _():
        for k in range(COLS // B):
            give(k).start()

    @pl.when((z == 0) | (idle == 1))
    def _():
        sent(0)
        sent(1)

    passed()
    for k in range(COLS // B):
        give(k).wait()


def on_device(matrix):
    return pl.pallas_call(
        kernel,
        out_shape=jax.ShapeDtypeStruct((ROWS, COLS), jnp.float32),
        in_specs=[pl.BlockSpec(memory_space=pltpu.HBM)],
        out_specs=pl.BlockSpec(memory_space=pl.ANY),
        scratch_shapes=[
            pltpu.VMEM((ROWS, COLS), jnp.float32),
            pltpu.VMEM((3 * ROWS + LAST * CH, COLS), jnp.float32),
            pltpu.VMEM((2, ROWS, B), jnp.float32),
            pltpu.VMEM((ROWS, B), jnp.float32),
            pltpu.VMEM((2 * B, COLS), jnp.bfloat16),
            pltpu.VMEM((2 * B, COLS), jnp.bfloat16),
            pltpu.SemaphoreType.DMA((2, 9)),
            pltpu.SemaphoreType.DMA((2, 2, NCH)),
            pltpu.SemaphoreType.DMA((2, 2)),
            pltpu.SemaphoreType.DMA((3,)),
            pltpu.SemaphoreType.DMA((2, NCZ)),
            pltpu.SemaphoreType.DMA((2,)),
            pltpu.SemaphoreType.DMA((COLS // B,)),
            pltpu.SemaphoreType.REGULAR,
        ],
        compiler_params=pltpu.CompilerParams(
            collective_id=0, has_side_effects=True, vmem_limit_bytes=VMEM
        ),
        name="panel_steps",
    )(matrix)


def solution(mesh):
    return jax.shard_map(
        on_device,
        mesh=mesh,
        in_specs=(P("row", "col"),),
        out_specs=P("row", "col"),
        check_vma=False,
    )
```

```python
import jax
import jax.numpy as jnp
from jax import lax
from jax.experimental import pallas as pl
from jax.experimental.pallas import tpu as pltpu
from jax.sharding import PartitionSpec as P

B = 256
ROWS, COLS = 144, 768
NX, NY, NZ = 4, 8, 12
CH = 8
NCH = ROWS // CH
CZ = 16
NCZ = ROWS // CZ
LAST = -(-(2 * B - 3 * ROWS) // CH)
PARTS = ((0, 2 * B), (2 * B, COLS - 2 * B))
MESH = pl.DeviceIdType.MESH
VMEM = 54500 << 10
F1, F2, FAR, EX, SIBP, SIBS, FAR2, G1, G2 = range(9)
RP, RX = range(2)
SP, SS = range(2)

Y_TREE = {0: (2, 6), 2: (3, 1), 6: (5, 7), 3: (4, None)}
Z_TREE = {
    0: (1, 9),
    1: (2, None),
    2: (3, None),
    3: (4, None),
    9: (6, 10),
    10: (11, None),
    6: (5, 7),
    7: (8, None),
}
HALF, HALF_FROM, HALF_PARENT = 8, 9, 7
EARLY = (5, 6)
PASS_FIRST = 9


def lookup(value, table):
    found = jnp.int32(0)
    entry = jnp.int32(0)
    for key, item in table.items():
        found = jnp.where(value == key, 1, found)
        entry = jnp.where(value == key, item, entry)
    return found, entry


def branch(tree, which):
    return {k: v[which] for k, v in tree.items() if v[which] is not None}


def parents(tree):
    return {child: k for k, v in tree.items() for child in v if child is not None}


def split(v):
    high = v.astype(jnp.bfloat16)
    low = (v - high.astype(jnp.float32)).astype(jnp.bfloat16)
    return high, low


def dot(a, b):
    return jnp.dot(a, b, preferred_element_type=jnp.float32)


def mult(a, b):
    ah, al = split(a)
    bh, bl = split(b)
    return dot(ah, bh) + (dot(ah, bl) + dot(al, bh))


def factors_of(block):
    i = lax.broadcasted_iota(jnp.int32, (B, B), 0)
    j = lax.broadcasted_iota(jnp.int32, (B, B), 1)
    diag = jnp.where(i == j, block, 0.0)
    two = jnp.where(i == j, 2.0, 0.0)
    across = 1.0 / jnp.sum(diag, axis=0, keepdims=True)
    down = 1.0 / jnp.sum(diag, axis=1, keepdims=True)
    return split(down * (two - block * across)), two


def times(a, pair):
    ah, al = split(a)
    return dot(ah, pair[0]) + (dot(ah, pair[1]) + dot(al, pair[0]))


def kernel(m_ref, o_ref, tile, ubuf, wbuf, low0, uhigh, ulow, ssem, rsem, ysem, zssem, zrsem, lsem, osem, zready):
    r = lax.axis_index("row")
    z = lax.axis_index("col")
    y, x, c = r // (2 * NX), (r // 2) % NX, r % 2
    odd = x % 2
    other = x + 1 - 2 * odd
    side = jnp.where((x == 1) | (x == 2), 1, 0)
    idle = jnp.where(r == 0, 1, 0)
    busy = 1 - idle

    def at(yy, xx, cc, zz):
        return ((yy * NX + xx) * 2 + cc, zz)

    has_f1, y1 = lookup(y, branch(Y_TREE, 0))
    has_f2, y2 = lookup(y, branch(Y_TREE, 1))
    has_up, yup = lookup(y, parents(Y_TREE))
    source = jnp.where((y == 0) & (x < 2), 1, 0)
    far_in = jnp.where((y == 0) & (x >= 2), 1, 0)
    has_z1, z1 = lookup(z, branch(Z_TREE, 0))
    has_z2, z2 = lookup(z, branch(Z_TREE, 1))
    has_zup, zup = lookup(z, parents(Z_TREE))
    has_z1, has_z2, has_zup = has_z1 * busy, has_z2 * busy, has_zup * busy
    early, _ = lookup(z, {k: 0 for k in EARLY})
    early1, _ = lookup(z1, {k: 0 for k in EARLY})
    early2, _ = lookup(z2, {k: 0 for k in EARLY})
    early1, early2 = has_z1 * early1, has_z2 * early2
    late1, late2 = has_z1 - early1, has_z2 - early2
    gives_half = jnp.where(z == HALF_FROM, busy, 0)
    xfar = NX - 1 - x
    straight = jnp.where((z == 0) & (r == 0), 1, 0)
    third = jnp.where((z == 0) & (c == 0) & (x == 2), 1, 0)
    has_ex = jnp.where((z == 0) & (c == 0) & (x == 3), 0, 1)
    has_sib = jnp.where(r == 1, 0, 1)

    mine = c + 2 * side
    theirs = c + 2 - 2 * side
    n_mine = jnp.where(mine == 3, LAST, NCH)
    n_theirs = jnp.where(theirs == 3, LAST, NCH)
    sib_p = 1 - c + 2 * side
    sib_s = 1 - c + 2 - 2 * side

    load = pltpu.make_async_copy(m_ref, tile, lsem.at[0])
    load.start()
    full = (source == 1) & (mine != 3)
    part = (source == 1) & (mine == 3)

    def own(n):
        return pltpu.make_async_copy(
            m_ref.at[pl.ds(0, n)], ubuf.at[pl.ds(pl.multiple_of(mine * ROWS, 8), n)], lsem.at[1]
        )

    @pl.when(full)
    def _():
        own(ROWS).start()

    @pl.when(part)
    def _():
        own(LAST * CH).start()

    bar = pltpu.get_barrier_semaphore()

    def hello(where):
        pl.semaphore_signal(bar, inc=1, device_id=where, device_id_type=MESH)

    @pl.when(has_up == 1)
    def _():
        hello(at(yup, x, c, z))

    @pl.when(far_in == 1)
    def _():
        hello(at(0, xfar, c, z))

    @pl.when((has_zup == 1) & (early == 1))
    def _():
        hello((r, zup))

    @pl.when((z == HALF) & (busy == 1))
    def _():
        hello((r, HALF_FROM))

    @pl.when(late1 == 1)
    def _():
        hello((r, z1))

    @pl.when(late2 == 1)
    def _():
        hello((r, z2))

    @pl.when(busy == 1)
    def _():
        hello(at(y, x, 1 - c, z))

    @pl.when((busy == 1) & (third == 0))
    def _():
        hello(at(y, other, c, z))

    @pl.when((third == 1) & (r == 4))
    def _():
        hello((0, z))

    @pl.when(r == 1)
    def _():
        hello((2, z))

    greeted = jnp.where((has_zup == 1) & (early == 0), 1, 0)
    pl.semaphore_wait(bar, has_ex + straight + has_sib + has_f1 + has_f2 + source + early1 + early2 + gives_half + greeted)

    @pl.when(greeted == 1)
    def _():
        pl.semaphore_signal(zready, inc=1, device_id=(r, zup), device_id_type=MESH)

    def rows_of(block, i):
        return pl.ds(pl.multiple_of(block * ROWS + i * CH, 8), CH)

    def moved(p, rows, kind, recv, where, src=None):
        ref = ubuf.at[rows, pl.ds(*PARTS[p])]
        return pltpu.make_async_remote_copy(
            src_ref=ref if src is None else src,
            dst_ref=ref,
            send_sem=ssem.at[p, kind],
            recv_sem=recv,
            device_id=where,
            device_id_type=MESH,
        )

    def whole(p, block, act):
        def of(n):
            act(pl.ds(pl.multiple_of(block * ROWS, 8), n))

        pl.when(block != 3)(lambda: of(ROWS))
        pl.when(block == 3)(lambda: of(LAST * CH))

    sibling = at(y, x, 1 - c, z)
    sends = (
        (F1, has_f1, RP, at(y1, x, c, z)),
        (F2, has_f2, RP, at(y2, x, c, z)),
        (FAR, source, RP, at(0, xfar, c, z)),
        (FAR2, straight, RX, (4, z)),
    )
    ex_to = at(y, other, c, z)
    plain_ex = (has_ex == 1) & (r != 2) & (straight == 0)
    onward = (
        (G1, third * has_f1, at(y1, x, c, z)),
        (G2, third * has_f2, at(y2, x, c, z)),
    )

    def first(p):
        def issue(i, own):
            rows = rows_of(mine, i)
            src = m_ref.at[rows_of(0, i), pl.ds(*PARTS[p])] if own else None
            for kind, has, got, where in sends if own else sends[:2]:

                @pl.when(has == 1)
                def _(kind=kind, got=got, where=where):
                    moved(p, rows, kind, rsem.at[p, got, i], where, src).start()

            @pl.when(plain_ex if own else has_ex == 1)
            def _():
                moved(p, rows, EX, rsem.at[p, RX, i], ex_to, src).start()

            if not own:
                moved(p, rows, SIBP, ysem.at[p, SP], sibling).start()
                return

            @pl.when(r == 2)
            def _():
                moved(p, rows, EX, ysem.at[p, SS], (1, z), src).start()

            @pl.when((has_sib == 1) & (straight == 0))
            def _():
                moved(p, rows, SIBP, ysem.at[p, SP], sibling, src).start()

        def body(i, carry):
            @pl.when(source == 1)
            def _():
                issue(i, True)

            @pl.when(source == 0)
            def _():
                moved(p, rows_of(mine, i), F1, rsem.at[p, RP, i], sibling).wait_recv()
                issue(i, False)

            return carry

        lax.fori_loop(0, n_mine, body, 0)

        @pl.when(straight == 1)
        def _():
            def exchange(i, carry):
                src = m_ref.at[rows_of(0, i), pl.ds(*PARTS[p])]
                moved(p, rows_of(mine, i), EX, rsem.at[p, RX, i], ex_to, src).start()
                moved(p, rows_of(mine, i), SIBP, ysem.at[p, SP], sibling, src).start()
                return carry

            lax.fori_loop(0, NCH, exchange, 0)

    def second(p):
        def body(i, carry):
            rows = rows_of(theirs, i)
            moved(p, rows, SIBS, rsem.at[p, RX, i], sibling).wait_recv()

            @pl.when(third == 1)
            def _():
                for kind, has, where in onward:

                    @pl.when(has == 1)
                    def _(kind=kind, where=where):
                        moved(p, rows, kind, rsem.at[p, RX, i], where).start()

            @pl.when(has_sib == 1)
            def _():
                moved(p, rows, SIBS, ysem.at[p, SS], sibling).start()

            return carry

        @pl.when(busy == 1)
        def _():
            lax.fori_loop(0, n_theirs, body, 0)
            whole(p, sib_p, lambda rows: moved(p, rows, SIBP, ysem.at[p, SP], sibling).wait_recv())
            whole(p, sib_s, lambda rows: moved(p, rows, SIBS, ysem.at[p, SS], sibling).wait_recv())

    def sent(p):
        def done(kind, block):
            whole(p, block, lambda rows: moved(p, rows, kind, rsem.at[p, RP, 0], sibling).wait_send())

        for kind, has, _, _ in sends:
            pl.when(has == 1)(lambda kind=kind: done(kind, mine))

        for kind, has, _ in onward:
            pl.when(has == 1)(lambda kind=kind: done(kind, theirs))

        pl.when(has_ex == 1)(lambda: done(EX, mine))
        pl.when(has_sib == 1)(lambda: done(SIBP, mine))
        pl.when((busy == 1) & (has_sib == 1))(lambda: done(SIBS, theirs))

    def wcopy(h, i, kind, where):
        ref = wbuf.at[h, pl.ds(pl.multiple_of(i * CZ, CZ), CZ)]
        return pltpu.make_async_remote_copy(
            src_ref=ref,
            dst_ref=ref,
            send_sem=zssem.at[kind],
            recv_sem=zrsem.at[h, i],
            device_id=where,
            device_id_type=MESH,
        )

    down = ((0, has_z1, (r, z1)), (1, has_z2, (r, z2)))

    def along(h):
        def body(i, carry):
            @pl.when(has_zup == 1)
            def _():
                wcopy(h, i, 0, (r, z1)).wait_recv()

            for kind, has, where in down:

                @pl.when(has == 1 if h == 1 else (has == 1) & (z != HALF_PARENT))
                def _(kind=kind, where=where):
                    wcopy(h, i, kind, where).start()

            return carry

        lax.fori_loop(0, NCZ, body, 0)

    def children():
        @pl.when(late1 + late2 > 0)
        def _():
            pl.semaphore_wait(zready, late1 + late2)

    def pass_on():
        children()
        along(1)
        along(0)

        @pl.when(gives_half == 1)
        def _():
            def body(i, carry):
                wcopy(0, i, 2, (r, HALF)).start()
                return carry

            lax.fori_loop(0, NCZ, body, 0)

    def passed():
        def gone(ref, kind):
            pltpu.make_async_remote_copy(
                src_ref=ref,
                dst_ref=ref,
                send_sem=zssem.at[kind],
                recv_sem=zrsem.at[0, 0],
                device_id=(r, z1),
                device_id_type=MESH,
            ).wait_send()

        pl.when((has_z1 == 1) & (z == HALF_PARENT))(lambda: gone(wbuf.at[1], 0))
        pl.when((has_z1 == 1) & (z != HALF_PARENT))(lambda: gone(wbuf, 0))
        pl.when(has_z2 == 1)(lambda: gone(wbuf, 1))
        pl.when(gives_half == 1)(lambda: gone(wbuf.at[0], 2))

    def give(k):
        cols = pl.ds(k * B, B)
        return pltpu.make_async_copy(tile.at[:, cols], o_ref.at[:, cols], osem.at[k])

    row_id = r * ROWS + lax.broadcasted_iota(jnp.int32, (ROWS, B), 0)
    below0 = row_id >= B
    below1 = row_id >= 2 * B

    ahead = (z != 0) | (source == 1)
    pass_first = (z == PASS_FIRST) & (busy == 1)
    first(0)

    pl.when(pass_first)(pass_on)

    @pl.when(ahead)
    def _():
        first(1)

    second(0)
    load.wait()

    @pl.when(full)
    def _():
        own(ROWS).wait()

    @pl.when(part)
    def _():
        own(LAST * CH).wait()

    @pl.when((z == 0) & (busy == 1))
    def _():
        first0, two = factors_of(ubuf[:B, :B])
        rest0 = split(two - times(ubuf[:B, :B], first0))
        l10 = times(times(ubuf[B : 2 * B, :B], first0), rest0)
        lower0 = times(times(tile[:, :B], first0), rest0)
        u01 = split(ubuf[:B, B : 2 * B])
        block1 = ubuf[B : 2 * B, B : 2 * B] - times(l10, u01)
        panel1 = tile[:, B : 2 * B] - times(lower0, u01)
        first1, _ = factors_of(block1)
        rest1 = split(two - times(block1, first1))
        lower1 = times(times(panel1, first1), rest1)
        wbuf[1] = jnp.where(below1, lower1, 0.0)
        children()
        along(1)
        w0 = lower0 - mult(lower1, l10)
        wbuf[0] = jnp.where(below1, w0, jnp.where(below0, lower0, 0.0))
        along(0)
        low0[...] = lower0
        tile[:, B : 2 * B] = jnp.where(below1, lower1, jnp.where(below0, panel1, tile[:, B : 2 * B]))

    @pl.when(jnp.logical_not(ahead))
    def _():
        first(1)

    second(1)

    def prepare():
        for start in range(0, COLS, B):
            uhigh[:, start : start + B], ulow[:, start : start + B] = split(ubuf[: 2 * B, start : start + B])

    def update(h):
        wh, wl = split(wbuf[h])
        for k in range(COLS // B):
            uh, ul = (u[h * B : (h + 1) * B, k * B : (k + 1) * B] for u in (uhigh, ulow))
            tile[:, k * B : (k + 1) * B] -= dot(wh, uh) + (dot(wh, ul) + dot(wl, uh))
            if h == 0:
                give(k).start()

    @pl.when((z != 0) & (busy == 1) & (has_z1 == 1))
    def _():
        sent(0)
        sent(1)
        pl.when(jnp.logical_not(pass_first))(pass_on)
        prepare()
        update(1)
        update(0)

    @pl.when((z != 0) & (busy == 1) & (has_z1 == 0))
    def _():
        prepare()
        sent(0)
        sent(1)
        along(1)
        update(1)
        along(0)
        update(0)

    @pl.when((z == 0) & (busy == 1))
    def _():
        for h in range(2):
            tile[:, 2 * B :] -= mult(wbuf[h], ubuf[h * B : (h + 1) * B, 2 * B :])

        tile[:, :B] = jnp.where(below0, low0[...], tile[:, :B])

    @pl.when((z == 0) | (idle == 1))
    def _():
        for k in range(COLS // B):
            give(k).start()

    @pl.when((z == 0) | (idle == 1))
    def _():
        sent(0)
        sent(1)

    passed()
    for k in range(COLS // B):
        give(k).wait()


def on_device(matrix):
    return pl.pallas_call(
        kernel,
        out_shape=jax.ShapeDtypeStruct((ROWS, COLS), jnp.float32),
        in_specs=[pl.BlockSpec(memory_space=pltpu.HBM)],
        out_specs=pl.BlockSpec(memory_space=pl.ANY),
        scratch_shapes=[
            pltpu.VMEM((ROWS, COLS), jnp.float32),
            pltpu.VMEM((3 * ROWS + LAST * CH, COLS), jnp.float32),
            pltpu.VMEM((2, ROWS, B), jnp.float32),
            pltpu.VMEM((ROWS, B), jnp.float32),
            pltpu.VMEM((2 * B, COLS), jnp.bfloat16),
            pltpu.VMEM((2 * B, COLS), jnp.bfloat16),
            pltpu.SemaphoreType.DMA((2, 9)),
            pltpu.SemaphoreType.DMA((2, 2, NCH)),
            pltpu.SemaphoreType.DMA((2, 2)),
            pltpu.SemaphoreType.DMA((3,)),
            pltpu.SemaphoreType.DMA((2, NCZ)),
            pltpu.SemaphoreType.DMA((2,)),
            pltpu.SemaphoreType.DMA((COLS // B,)),
            pltpu.SemaphoreType.REGULAR,
        ],
        compiler_params=pltpu.CompilerParams(
            collective_id=0, has_side_effects=True, vmem_limit_bytes=VMEM
        ),
        name="panel_steps",
    )(matrix)


def solution(mesh):
    return jax.shard_map(
        on_device,
        mesh=mesh,
        in_specs=(P("row", "col"),),
        out_specs=P("row", "col"),
        check_vma=False,
    )
```
